32 devices in a mesh: grp: 2 (over x), row: 16 (over z, y, core).
Axes of the slice: x: 2, y: 2, z: 4, core: 2. Of those that a mesh axis runs over, the one named last changes fastest.
Arguments:
- start_vectors: bfloat16 [64, 73728], P(None, ('grp', 'row')), parts along dimension 1, may hold values from -6 to 6
- blocks: bfloat16 [384, 12, 192, 192], P(('grp', 'row')), parts along dimension 0
- block_cols: int32 [384, 12], P(('grp', 'row')), parts along dimension 0, may hold values from 0 to 191, as said below
- positions: bfloat16 [73728], P(('grp', 'row')), parts along dimension 0, may hold values from -1 to 1
Outputs:
- chebyshev_two: bfloat16 [64, 73728], P(None, ('grp', 'row')), parts along dimension 1
- heat_current: float32 [64, 73728], P(None, ('grp', 'row')), parts along dimension 1
The draws below stay inside these ranges and needn't reach their ends.
There are 2 independent parts, one for each index of `grp`. The reference program is written for one: setup_inputs(seed, part) draws one part's arguments, and reference() takes and returns one part's arrays. A program takes and returns all parts, laid end to end along the dimension named above; each array names one. Nothing has to cross between parts.
Inputs may be any that keep to these rules, and one draw needn't show every extreme that they name: block_cols[c, 0] = c; the other entries of row c are distinct clusters (c + d) mod 192 with d from 1 to 12; some row holds distance 12.
All inputs are finite; a program needn't handle non-finite values.
Results may differ from the reference program's by a relative error of at most 0.012.
Values may be sent and summed in bfloat16 or wider, within the bound.
A program may use at most 128 MiB of HBM per device.

```python
import jax
import jax.numpy as jnp
from jax import lax

B = 192
NV = 64
NBR = 12
REACH = 12
NCL = 192
ROWS = 36864


def draw_blocks(key, part):
    key = jax.random.fold_in(key, 11)
    block_shape = (NCL, NBR, B, B)
    spread_factor = (4.0 * (2 * NBR - 1) * B) ** (-0.5)
    sampled = jax.random.normal(key, block_shape, jnp.float32)
    symmetric = (sampled[:, 0] + jnp.swapaxes(sampled[:, 0], 1, 2)) * 0.70710678
    sampled = sampled.at[:, 0].set(symmetric)
    return (sampled * spread_factor).astype(jnp.bfloat16)


def draw_block_cols(key, part):
    key = jax.random.fold_in(key, 23)
    cluster_keys = jax.random.split(key, NCL)
    shuffled = jax.vmap(lambda sub_key: jax.random.permutation(sub_key, REACH))(cluster_keys).astype(jnp.int32) + 1
    descending = REACH - jnp.arange(REACH, dtype=jnp.int32)
    cluster_ids = jnp.arange(NCL, dtype=jnp.int32)
    shuffled = jnp.where(cluster_ids[:, None] == 0, descending[None, :], shuffled)
    offsets = jnp.concatenate([jnp.zeros((NCL, 1), jnp.int32), shuffled[:, :NBR - 1]], axis=1)
    return jnp.mod(cluster_ids[:, None] + offsets, NCL).astype(jnp.int32)


def level_of(rng, extent, cuts, smallest, high):
    loudness = 1.0
    for position, parts in cuts:
        heights = jax.random.uniform(jax.random.fold_in(jax.random.fold_in(rng, 6), position), (parts,), jnp.float32, smallest / len(cuts), high / len(cuts))
        loudness = loudness * jnp.repeat(jnp.exp(heights), extent[position] // parts).reshape((-1,) + (1,) * (len(extent) - 1 - position))
    return loudness


def bell_draw(stream_key, extent, scale, reach, cuts=(), held_as=jnp.bfloat16):
    drawn = jax.random.normal(stream_key, extent, jnp.float32) * scale
    if len(cuts) > 0:
        drawn = level_of(stream_key, extent, cuts, -0.22, 0.18) * drawn
    return jnp.clip(drawn, min=-reach, max=reach).astype(held_as)


def setup_inputs(seed: int = 0, part: int = 0) -> dict:
    arg_keys = jax.random.split(jax.random.key(seed), 5)
    part_keys = jax.random.split(jax.random.fold_in(arg_keys[4], part), 5)
    start_vectors = bell_draw(part_keys[0], (NV, ROWS), 1.0, 6.0, ((1, 16),))
    blocks = draw_blocks(jax.random.fold_in(jax.random.fold_in(arg_keys[4], part), 71), part)
    block_cols = draw_block_cols(jax.random.fold_in(jax.random.fold_in(arg_keys[4], part), 71), part)
    positions = jnp.clip(jax.random.uniform(part_keys[3], (ROWS,), jnp.float32, -1.0, 1.0) * level_of(part_keys[3], (ROWS,), ((0, 16),), -0.4, 0.0), -1.0, 1.0).astype(jnp.bfloat16)
    return {"start_vectors": start_vectors, "blocks": blocks, "block_cols": block_cols, "positions": positions}


def apply_matrix(vectors, blocks, block_cols):
    vector_count = vectors.shape[0]
    clusters, slot_count, block_width, _ = blocks.shape
    panels = vectors.astype(jnp.float32).reshape(vector_count, clusters, block_width)
    running_sum = jnp.zeros((vector_count, clusters, block_width), jnp.float32)
    for slot_index in range(slot_count):
        matrix = blocks[:, slot_index].astype(jnp.float32)
        columns = block_cols[:, slot_index].astype(jnp.int32)
        running_sum = running_sum + jnp.einsum("njb,jab->nja", panels[:, columns], matrix)
        if slot_index > 0:
            running_sum = running_sum.at[:, columns].add(jnp.einsum("nja,jab->njb", panels, matrix))
    return running_sum.reshape(vector_count, -1)


def reference(start_vectors, blocks, block_cols, positions):
    vector_count = start_vectors.shape[0]
    first_step = lax.optimization_barrier(apply_matrix(start_vectors, blocks, block_cols).astype(jnp.bfloat16))
    second_step = 2.0 * apply_matrix(first_step, blocks, block_cols) - start_vectors.astype(jnp.float32)
    second_step = lax.optimization_barrier(second_step.astype(jnp.bfloat16))
    weights = positions.astype(jnp.float32)[None, :]
    scaled = (weights * second_step.astype(jnp.float32)).astype(jnp.bfloat16)
    stacked_result = apply_matrix(jnp.concatenate([second_step, scaled], axis=0), blocks, block_cols)
    heat_current = weights * stacked_result[:vector_count] - stacked_result[vector_count:]
    return second_step, heat_current
```

```python
import functools

import jax
import jax.numpy as jnp
from jax import lax
from jax.experimental import pallas as pl
from jax.experimental.pallas import tpu as pltpu
from jax.sharding import PartitionSpec as P

F32 = jnp.float32
BF16 = jnp.bfloat16
NT = (((1,), (1,)), ((), ()))


def kernel(table, v_ref, p_ref, blocks_ref, x2_ref, heat_ref,
           blk, z0, e0, z1, e1, z2, e2, own, sout, sin, pup,
           blk_sem, vs_sem, vr_sem, ss_sem, sr_sem, ps_sem, pr_sem):
    C, K = blocks_ref.shape[0], blocks_ref.shape[1]
    B = blocks_ref.shape[2]
    NV = v_ref.shape[0]
    n = lax.axis_size("row")
    me = lax.axis_index("row")
    nxt, prv = lax.rem(me + 1, n), lax.rem(me + n - 1, n)

    def block_copy(i):
        return pltpu.make_async_copy(
            blocks_ref.at[i], blk.at[i, pl.ds(0, K)], blk_sem.at[i])

    for i in range(C):
        block_copy(i).start()

    barrier = pltpu.get_barrier_semaphore()
    for neighbour in (prv, nxt):
        pl.semaphore_signal(barrier, inc=1, device_id={"row": neighbour},
                            device_id_type=pl.DeviceIdType.MESH)

    @pl.loop(0, C)
    def _(i):
        blk[i, K] = jnp.zeros((B, B), BF16)
        for z in (z0, z1, z2):
            z[i] = jnp.zeros(z.shape[1:], BF16)
            z[2 * C + i] = jnp.zeros(z.shape[1:], BF16)

    for t in range(C // 2):
        pair = v_ref[:, 2 * t * B:2 * (t + 1) * B]
        for h in range(2):
            panel = pair[:, h * B:(h + 1) * B]
            e0[2 * t + h] = panel
            z0[C + 2 * t + h] = panel

    pl.semaphore_wait(barrier, 2)

    def vec_copy(app, i):
        e = (e0, e1, e2)[app]
        return pltpu.make_async_remote_copy(
            src_ref=e.at[i, pl.ds(0, NV)], dst_ref=e.at[C + i, pl.ds(0, NV)],
            send_sem=vs_sem.at[app, i], recv_sem=vr_sem.at[app, i],
            device_id={"row": prv}, device_id_type=pl.DeviceIdType.MESH)

    def spill_copy(app, j):
        return pltpu.make_async_remote_copy(
            src_ref=sout.at[app, j], dst_ref=sin.at[app, j],
            send_sem=ss_sem.at[app, j], recv_sem=sr_sem.at[app, j],
            device_id={"row": nxt}, device_id_type=pl.DeviceIdType.MESH)

    @pl.loop(0, C)
    def _(i):
        vec_copy(0, i).start()

    pos_copy = pltpu.make_async_remote_copy(
        src_ref=p_ref, dst_ref=pup, send_sem=ps_sem, recv_sem=pr_sem,
        device_id={"row": prv}, device_id_type=pl.DeviceIdType.MESH)
    pos_copy.start()

    for i in range(C):
        block_copy(i).wait()

    for app, (z, e) in enumerate(((z0, e0), (z1, e1), (z2, e2))):
        M = z.shape[1]
        if app == 2:
            pos_copy.wait()

        @pl.loop(0, C)
        def _(j):
            acc = jnp.zeros((2 * M, B), F32)
            for d in range(1, K + 1):
                i = lax.rem(j + C - d, C)
                lhs = jnp.concatenate([z[C + j - d], z[2 * C + j - d]], axis=0)
                acc = acc + jnp.dot(lhs, blk[i, table[i, d]],
                                    preferred_element_type=F32)
            own[j, :M] = acc[:M]
            spill = acc[M:]
            if app == 2:
                spill = pup[pl.ds(j, 1), :] * spill[:NV] - spill[NV:]
            sout[app, j] = spill.astype(BF16)
            spill_copy(app, j).start()

        @pl.loop(0, C)
        def _(i):
            vec_copy(app, i).wait_recv()
            if app == 2:
                up = pup[pl.ds(i, 1), :] * e[C + i, :NV].astype(F32)
                e[C + i, NV:] = up.astype(BF16)
            acc = own[i, :M]
            for d in range(K + 1):
                acc = acc + lax.dot_general(e[i + d], blk[i, table[i, d]], NT,
                                            preferred_element_type=F32)
            spill_copy(app, i).wait_recv()
            arriving = sin[app, i].astype(F32)
            if app == 0:
                x1 = (acc + arriving).astype(BF16)
                e1[i] = x1
                z1[C + i] = x1
                vec_copy(1, i).start()
            elif app == 1:
                h = acc + arriving
                x2 = (2.0 * h - e0[i].astype(F32)).astype(BF16)
                e2[i, :NV] = x2
                vec_copy(2, i).start()
                z2[C + i, :NV] = x2
                scaled = (p_ref[pl.ds(i, 1), :] * x2.astype(F32)).astype(BF16)
                e2[i, NV:] = scaled
                z2[C + i, NV:] = scaled
            else:
                weight = p_ref[pl.ds(i, 1), :]
                own[i, :NV] = weight * acc[:NV] - acc[NV:] + arriving

    for t in range(C // 2):
        cols = slice(2 * t * B, 2 * (t + 1) * B)
        x2_ref[:, cols] = jnp.concatenate(
            [e2[2 * t, :NV], e2[2 * t + 1, :NV]], axis=1)
        heat_ref[:, cols] = jnp.concatenate(
            [own[2 * t, :NV], own[2 * t + 1, :NV]], axis=1)

    for app in range(3):
        @pl.loop(0, C)
        def _(i):
            vec_copy(app, i).wait_send()
            spill_copy(app, i).wait_send()


def body(start_vectors, blocks, block_cols, positions):
    C, K, B = blocks.shape[0], blocks.shape[1], blocks.shape[2]
    NV = start_vectors.shape[0]
    clusters = C * lax.axis_size("row")
    first = lax.axis_index("row") * C
    row_ids = first + jnp.arange(C, dtype=jnp.int32)
    offsets = jnp.mod(block_cols - row_ids[:, None], clusters)
    distance = jnp.arange(K + 1, dtype=jnp.int32)
    slots = jnp.arange(K, dtype=jnp.int32)
    table = K + jnp.sum(
        jnp.where(offsets[:, :, None] == distance, slots[None, :, None] - K, 0), axis=1)
    rows = -(-C // 16) * 16
    weights = jnp.pad(positions.astype(F32).reshape(C, B), ((0, rows - C), (0, 0)))
    vmem = pl.BlockSpec(memory_space=pltpu.VMEM)
    dma = pltpu.SemaphoreType.DMA
    return tuple(pl.pallas_call(
        kernel,
        out_shape=(jax.ShapeDtypeStruct(start_vectors.shape, BF16),
                   jax.ShapeDtypeStruct(start_vectors.shape, F32)),
        in_specs=[pl.BlockSpec(memory_space=pltpu.SMEM), vmem, vmem,
                  pl.BlockSpec(memory_space=pl.ANY)],
        out_specs=(vmem, vmem),
        scratch_shapes=[
            pltpu.VMEM((C, K + 1, B, B), BF16),
            pltpu.VMEM((3 * C, NV, B), BF16), pltpu.VMEM((2 * C, NV, B), BF16),
            pltpu.VMEM((3 * C, NV, B), BF16), pltpu.VMEM((2 * C, NV, B), BF16),
            pltpu.VMEM((3 * C, 2 * NV, B), BF16), pltpu.VMEM((2 * C, 2 * NV, B), BF16),
            pltpu.VMEM((C, 2 * NV, B), F32),
            pltpu.VMEM((3, C, NV, B), BF16), pltpu.VMEM((3, C, NV, B), BF16),
            pltpu.VMEM((rows, B), F32),
            dma((C,)), dma((3, C)), dma((3, C)), dma((3, C)), dma((3, C)), dma, dma,
        ],
        compiler_params=pltpu.CompilerParams(
            collective_id=0, has_side_effects=True, vmem_limit_bytes=56 * 1024 * 1024),
    )(table.astype(jnp.int32), start_vectors, weights, blocks))


def solution(mesh):
    return jax.shard_map(
        body,
        mesh=mesh,
        in_specs=(
            P(None, ("grp", "row")),
            P(("grp", "row"), None, None, None),
            P(("grp", "row"), None),
            P(("grp", "row")),
        ),
        out_specs=(P(None, ("grp", "row")), P(None, ("grp", "row"))),
        check_vma=False,
    )
```

```python
import jax
import jax.numpy as jnp
from jax import lax
from jax.experimental import pallas as pl
from jax.experimental.pallas import tpu as pltpu
from jax.sharding import PartitionSpec as P

F32 = jnp.float32
BF16 = jnp.bfloat16
STEP = 4


def kernel(cols_ref, v_ref, p_ref, blocks_ref, x2_ref, heat_ref,
           blk, blkt, ze, zo, ee0, eo0, ee1, eo1, ee2, eo2, own, sout, sin,
           pos, pup, tabv, table,
           blk_sem, vs_sem, vr_sem, ss_sem, sr_sem, ps_sem, pr_sem, tab_sem):
    C, K = blocks_ref.shape[0], blocks_ref.shape[1]
    B = blocks_ref.shape[2]
    NV = v_ref.shape[0]
    Q = C // 2
    W = 2 * B
    n = lax.axis_size("row")
    me = lax.axis_index("row")
    nxt, prv = lax.rem(me + 1, n), lax.rem(me + n - 1, n)

    barrier = pltpu.get_barrier_semaphore()
    for neighbour in (prv, nxt):
        pl.semaphore_signal(barrier, inc=1, device_id={"row": neighbour},
                            device_id_type=pl.DeviceIdType.MESH)

    def block_copy(i):
        return pltpu.make_async_copy(
            blocks_ref.at[i], blk.at[i, pl.ds(0, K)], blk_sem.at[i])

    for i in range(C):
        block_copy(i).start()

    clusters = C * n
    off = cols_ref[...] - (me * C + lax.broadcasted_iota(jnp.int32, (C, K), 0))
    off = jnp.where(off < 0, off + clusters, off)
    lane = lax.broadcasted_iota(jnp.int32, (C, 128), 1)
    found = jnp.full((C, 128), K, jnp.int32)
    for k in range(K):
        found = jnp.where(off[:, k:k + 1] == lane, k, found)
    tabv[...] = found
    table_copy = pltpu.make_async_copy(tabv, table, tab_sem)
    table_copy.start()

    for q in range(Q):
        pair = v_ref[:, q * W:(q + 1) * W]
        ee0[q] = pair
        ze[Q + q, :NV] = pair
    pos[...] = jnp.zeros(pos.shape, F32)
    for q in range(Q):
        pos[q:q + 1, :] = p_ref[:, q * W:(q + 1) * W].astype(F32)

    def vec_copy(app, q):
        e = (ee0, ee1, ee2)[app]
        return pltpu.make_async_remote_copy(
            src_ref=e.at[q, pl.ds(0, NV)], dst_ref=e.at[Q + q, pl.ds(0, NV)],
            send_sem=vs_sem.at[app, q], recv_sem=vr_sem.at[app, q],
            device_id={"row": prv}, device_id_type=pl.DeviceIdType.MESH)

    def spill_copy(app, q):
        return pltpu.make_async_remote_copy(
            src_ref=sout.at[app, q], dst_ref=sin.at[app, q],
            send_sem=ss_sem.at[app, q], recv_sem=sr_sem.at[app, q],
            device_id={"row": nxt}, device_id_type=pl.DeviceIdType.MESH)

    pl.semaphore_wait(barrier, 2)
    for q in range(Q):
        vec_copy(0, q).start()
    pos_copy = pltpu.make_async_remote_copy(
        src_ref=pos, dst_ref=pup, send_sem=ps_sem, recv_sem=pr_sem,
        device_id={"row": prv}, device_id_type=pl.DeviceIdType.MESH)
    pos_copy.start()

    def straddle(ref, q, rows):
        return jnp.concatenate([ref[q, :rows, B:], ref[q + 1, :rows, :B]], axis=1)

    for q in range(Q):
        ze[q] = jnp.zeros(ze.shape[1:], BF16)
        ze[2 * Q + q] = jnp.zeros(ze.shape[1:], BF16)
        if q < Q - 1:
            zo[q] = jnp.zeros(zo.shape[1:], BF16)
            zo[2 * Q + q] = jnp.zeros(zo.shape[1:], BF16)

    def odd_pairs(rows, eo):
        for q in range(Q - 1, 2 * Q):
            odd = straddle(ze, q, rows)
            zo[q, :rows] = odd
            if Q <= q < 2 * Q - 1:
                eo[q - Q] = odd

    odd_pairs(NV, eo0)

    for i in range(C):
        blk[i, K] = jnp.zeros((B, B), BF16)
        blkt[i, K] = jnp.zeros((B, B), BF16)

    @pl.loop(0, C)
    def _(i):
        block_copy(i).wait()
        for k in range(K):
            blkt[i, k] = blk[i, k].T

    table_copy.wait()

    def across(ref, start, rows):
        return [ref[start + m, :rows] for m in range(Q)]

    for app, (ee, eo) in enumerate(((ee0, eo0), (ee1, eo1), (ee2, eo2))):
        M = 2 * NV if app == 2 else NV
        if app == 2:
            pos_copy.wait()

        @pl.loop(0, C // STEP)
        def _(s):
            spills = []
            for h in range(STEP):
                j = STEP * s + h
                t = (STEP // 2) * s + h // 2
                z = (ze, zo)[h % 2]
                lhs = jnp.concatenate(
                    [jnp.concatenate(across(z, t, M), axis=1),
                     jnp.concatenate(across(z, t + Q, M), axis=1)], axis=0)
                rows = [lax.rem(j + C - d, C) for d in range(K, 0, -1)]
                rhs = jnp.concatenate(
                    [blk[i, table[i, K - m]] for m, i in enumerate(rows)], axis=0)
                acc = jnp.dot(lhs, rhs, preferred_element_type=F32)
                own[j, :M] = acc[:M]
                spills.append(acc[M:])
            for g in range(STEP // 2):
                q = (STEP // 2) * s + g
                spill = jnp.concatenate(spills[2 * g:2 * g + 2], axis=1)
                if app == 2:
                    spill = pup[pl.ds(q, 1), :] * spill[:NV] - spill[NV:]
                sout[app, q] = spill.astype(BF16)
                spill_copy(app, q).start()

        @pl.loop(0, C // STEP)
        def _(s):
            for g in range(STEP // 2):
                q = (STEP // 2) * s + g
                vec_copy(app, q).wait_recv()
                if app == 2:
                    up = pup[pl.ds(q, 1), :] * ee[Q + q, :NV].astype(F32)
                    ee[Q + q, NV:] = up.astype(BF16)
                eo[Q - 1 + q] = straddle(ee, Q - 1 + q, M)
            sums = []
            for h in range(STEP):
                j = STEP * s + h
                t = (STEP // 2) * s + h // 2
                last = ee[t + Q]
                last = last[:, B:] if h % 2 else last[:, :B]
                lhs = jnp.concatenate(
                    across((ee, eo)[h % 2], t, M) + [last], axis=1)
                rhs = jnp.concatenate(
                    [blkt[j, table[j, d]] for d in range(K + 1)], axis=0)
                sums.append(own[j, :M] + jnp.dot(
                    lhs, rhs, preferred_element_type=F32))
            for g in range(STEP // 2):
                q = (STEP // 2) * s + g
                total = jnp.concatenate(sums[2 * g:2 * g + 2], axis=1)
                spill_copy(app, q).wait_recv()
                arriving = sin[app, q].astype(F32)
                if app == 0:
                    x1 = (total + arriving).astype(BF16)
                    ee1[q] = x1
                    vec_copy(1, q).start()
                    ze[Q + q, :NV] = x1
                elif app == 1:
                    x2 = 2.0 * (total + arriving) - ee0[q].astype(F32)
                    x2 = x2.astype(BF16)
                    ee2[q, :NV] = x2
                    vec_copy(2, q).start()
                    scaled = (pos[pl.ds(q, 1), :] * x2.astype(F32)).astype(BF16)
                    ee2[q, NV:] = scaled
                    ze[Q + q, :NV] = x2
                    ze[Q + q, NV:] = scaled
                    x2_ref[:, pl.ds(pl.multiple_of(q * W, 128), W)] = x2
                else:
                    weight = pos[pl.ds(q, 1), :]
                    heat = weight * total[:NV] - total[NV:] + arriving
                    heat_ref[:, pl.ds(pl.multiple_of(q * W, 128), W)] = heat

        if app == 0:
            odd_pairs(NV, eo1)
        elif app == 1:
            odd_pairs(2 * NV, eo2)

    for app in range(3):
        for q in range(Q):
            vec_copy(app, q).wait_send()
            spill_copy(app, q).wait_send()


def body(start_vectors, blocks, block_cols, positions):
    C, K, B = blocks.shape[0], blocks.shape[1], blocks.shape[2]
    NV = start_vectors.shape[0]
    Q, W = C // 2, 2 * B
    rows = -(-Q // 8) * 8
    vmem = pl.BlockSpec(memory_space=pltpu.VMEM)
    dma = pltpu.SemaphoreType.DMA
    pairs = lambda count, m: pltpu.VMEM((count, m, W), BF16)
    return tuple(pl.pallas_call(
        kernel,
        out_shape=(jax.ShapeDtypeStruct(start_vectors.shape, BF16),
                   jax.ShapeDtypeStruct(start_vectors.shape, F32)),
        in_specs=[vmem, vmem, vmem, pl.BlockSpec(memory_space=pl.ANY)],
        out_specs=(vmem, vmem),
        scratch_shapes=[
            pltpu.VMEM((C, K + 1, B, B), BF16), pltpu.VMEM((C, K + 1, B, B), BF16),
            pairs(3 * Q, 2 * NV), pairs(3 * Q, 2 * NV),
            pairs(2 * Q, NV), pairs(2 * Q, NV),
            pairs(2 * Q, NV), pairs(2 * Q, NV),
            pairs(2 * Q, 2 * NV), pairs(2 * Q, 2 * NV),
            pltpu.VMEM((C, 2 * NV, B), F32),
            pltpu.VMEM((3, Q, NV, W), BF16), pltpu.VMEM((3, Q, NV, W), BF16),
            pltpu.VMEM((rows, W), F32), pltpu.VMEM((rows, W), F32),
            pltpu.VMEM((C, 128), jnp.int32), pltpu.SMEM((C, 128), jnp.int32),
            dma((C,)), dma((3, Q)), dma((3, Q)), dma((3, Q)), dma((3, Q)),
            dma, dma, dma,
        ],
        compiler_params=pltpu.CompilerParams(
            collective_id=0, has_side_effects=True, vmem_limit_bytes=56 * 1024 * 1024),
    )(block_cols, start_vectors, positions.reshape(1, -1), blocks))


def solution(mesh):
    return jax.shard_map(
        body,
        mesh=mesh,
        in_specs=(
            P(None, ("grp", "row")),
            P(("grp", "row"), None, None, None),
            P(("grp", "row"), None),
            P(("grp", "row")),
        ),
        out_specs=(P(None, ("grp", "row")), P(None, ("grp", "row"))),
        check_vma=False,
    )
```

```python
import jax
import jax.numpy as jnp
from jax import lax
from jax.experimental import pallas as pl
from jax.experimental.pallas import tpu as pltpu
from jax.sharding import PartitionSpec as P

F32 = jnp.float32
BF16 = jnp.bfloat16
STEP = 6
GROUP = 2
LATE = True


def kernel(cols_ref, v_ref, p_ref, blocks_ref, x2_ref, heat_ref,
           blk, blkt, ze, zo, ee0, eo0, ee1, eo1, ee2, eo2, own, sout, sin,
           pos, pup, tabv, table,
           blk_sem, vs_sem, vr_sem, ss_sem, sr_sem, ps_sem, pr_sem, tab_sem):
    C, K = blocks_ref.shape[0], blocks_ref.shape[1]
    B = blocks_ref.shape[2]
    NV = v_ref.shape[0]
    Q = C // 2
    W = 2 * B
    n = lax.axis_size("row")
    me = lax.axis_index("row")
    nxt, prv = lax.rem(me + 1, n), lax.rem(me + n - 1, n)

    barrier = pltpu.get_barrier_semaphore()
    for neighbour in (prv, nxt):
        pl.semaphore_signal(barrier, inc=1, device_id={"row": neighbour},
                            device_id_type=pl.DeviceIdType.MESH)

    def block_copy(i):
        return pltpu.make_async_copy(
            blocks_ref.at[i], blk.at[i, pl.ds(0, K)], blk_sem.at[i])

    for i in range(C):
        block_copy(i).start()

    clusters = C * n
    off = cols_ref[...] - (me * C + lax.broadcasted_iota(jnp.int32, (C, K), 0))
    off = jnp.where(off < 0, off + clusters, off)
    lane = lax.broadcasted_iota(jnp.int32, (C, 128), 1)
    found = jnp.full((C, 128), K, jnp.int32)
    for k in range(K):
        found = jnp.where(off[:, k:k + 1] == lane, k, found)
    tabv[...] = found
    table_copy = pltpu.make_async_copy(tabv, table, tab_sem)
    table_copy.start()

    for q in range(Q):
        pair = v_ref[:, q * W:(q + 1) * W]
        ee0[q] = pair
        ze[Q + q, :NV] = pair
    pos[...] = jnp.zeros(pos.shape, F32)
    lines = p_ref[...].astype(F32)
    for q in range(Q):
        pos[q:q + 1, :] = jnp.concatenate(
            [lines[r:r + 1] for r in range(q * W // 128, (q + 1) * W // 128)], axis=1)

    def vec_copy(app, q):
        e = (ee0, ee1, ee2)[app]
        return pltpu.make_async_remote_copy(
            src_ref=e.at[q, pl.ds(0, NV)], dst_ref=e.at[Q + q, pl.ds(0, NV)],
            send_sem=vs_sem.at[app, q], recv_sem=vr_sem.at[app, q],
            device_id={"row": prv}, device_id_type=pl.DeviceIdType.MESH)

    def spill_copy(app, q):
        return pltpu.make_async_remote_copy(
            src_ref=sout.at[app, q], dst_ref=sin.at[app, q],
            send_sem=ss_sem.at[app, q], recv_sem=sr_sem.at[app, q],
            device_id={"row": nxt}, device_id_type=pl.DeviceIdType.MESH)

    pl.semaphore_wait(barrier, 2)
    for q in range(Q):
        vec_copy(0, q).start()
    pos_copy = pltpu.make_async_remote_copy(
        src_ref=pos, dst_ref=pup, send_sem=ps_sem, recv_sem=pr_sem,
        device_id={"row": prv}, device_id_type=pl.DeviceIdType.MESH)
    pos_copy.start()

    def straddle(ref, q, rows):
        return jnp.concatenate([ref[q, :rows, B:], ref[q + 1, :rows, :B]], axis=1)

    for q in range(Q):
        ze[q] = jnp.zeros(ze.shape[1:], BF16)
        ze[2 * Q + q] = jnp.zeros(ze.shape[1:], BF16)
        if q < Q - 1:
            zo[q] = jnp.zeros(zo.shape[1:], BF16)
            zo[2 * Q + q] = jnp.zeros(zo.shape[1:], BF16)

    def odd_pairs(rows, eo):
        for q in range(Q - 1, 2 * Q):
            odd = straddle(ze, q, rows)
            zo[q, :rows] = odd
            if Q <= q < 2 * Q - 1:
                eo[q - Q] = odd

    odd_pairs(NV, eo0)

    for i in range(C):
        blk[i, K] = jnp.zeros((B, B), BF16)
        blkt[i, K] = jnp.zeros((B, B), BF16)

    @pl.loop(0, C)
    def _(i):
        block_copy(i).wait()
        for k in range(K):
            blkt[i, k] = blk[i, k].T

    table_copy.wait()

    def across(ref, start, rows):
        return [ref[start + m, :rows] for m in range(Q)]

    for app, (ee, eo) in enumerate(((ee0, eo0), (ee1, eo1), (ee2, eo2))):
        M = 2 * NV if app == 2 else NV
        if app == 2:
            pos_copy.wait()

        if app < 2:
            @pl.loop(0, C // STEP)
            def _(s):
                spills = []
                for h in range(STEP):
                    j = STEP * s + h
                    t = (STEP // 2) * s + h // 2
                    z = (ze, zo)[h % 2]
                    lhs = jnp.concatenate(
                        [jnp.concatenate(across(z, t, M), axis=1),
                         jnp.concatenate(across(z, t + Q, M), axis=1)], axis=0)
                    rows = [lax.rem(j + C - d, C) for d in range(K, 0, -1)]
                    rhs = jnp.concatenate(
                        [blk[i, table[i, K - m]] for m, i in enumerate(rows)], axis=0)
                    acc = jnp.dot(lhs, rhs, preferred_element_type=F32)
                    own[j, :M] = acc[:M]
                    spills.append(acc[M:])
                for g in range(STEP // 2):
                    q = (STEP // 2) * s + g
                    spill = jnp.concatenate(spills[2 * g:2 * g + 2], axis=1)
                    sout[app, q] = spill.astype(BF16)
                    spill_copy(app, q).start()

        else:
            def mirrored(j, low, high):
                count = high - low
                src = eo if low % 2 else ee
                parts = [src[low // 2 + m] for m in range(count // 2)]
                if count % 2:
                    last = ee[(high - 1) // 2]
                    parts.append(last[:, :B] if high % 2 else last[:, B:])
                lhs = jnp.concatenate(parts, axis=1)
                rhs = jnp.concatenate(
                    [blk[i, table[i, (j - i) % C if j != i else C]]
                     for i in range(low, high)], axis=0)
                return jnp.dot(lhs, rhs, preferred_element_type=F32)

            for q in range(Q):
                pair = []
                for j in (2 * q, 2 * q + 1):
                    pair.append(mirrored(j, j, C))
                    if j:
                        own[j] = mirrored(j, 0, j)
                    else:
                        own[j] = jnp.zeros(own.shape[1:], F32)
                spill = jnp.concatenate(pair, axis=1)
                spill = pup[q:q + 1, :] * spill[:NV] - spill[NV:]
                sout[app, q] = spill.astype(BF16)
                spill_copy(app, q).start()

        def products(s):
            for g in range(GROUP // 2):
                q = (GROUP // 2) * s + g
                vec_copy(app, q).wait_recv()
                if app == 2:
                    up = pup[q:q + 1, :] * ee[Q + q, :NV].astype(F32)
                    ee[Q + q, NV:] = up.astype(BF16)
                eo[Q - 1 + q] = straddle(ee, Q - 1 + q, M)
            sums = []
            for h in range(GROUP):
                j = GROUP * s + h
                t = (GROUP // 2) * s + h // 2
                last = ee[t + Q]
                last = last[:, B:] if h % 2 else last[:, :B]
                lhs = jnp.concatenate(
                    across((ee, eo)[h % 2], t, M) + [last], axis=1)
                rhs = jnp.concatenate(
                    [blkt[j, table[j, d]] for d in range(K + 1)], axis=0)
                sums.append(own[j, :M] + jnp.dot(
                    lhs, rhs, preferred_element_type=F32))
            return sums

        def finish(s, sums):
            for g in range(GROUP // 2):
                q = (GROUP // 2) * s + g
                total = jnp.concatenate(sums[2 * g:2 * g + 2], axis=1)
                spill_copy(app, q).wait_recv()
                arriving = sin[app, q].astype(F32)
                if app == 0:
                    x1 = (total + arriving).astype(BF16)
                    ee1[q] = x1
                    vec_copy(1, q).start()
                    ze[Q + q, :NV] = x1
                elif app == 1:
                    x2 = 2.0 * (total + arriving) - ee0[q].astype(F32)
                    x2 = x2.astype(BF16)
                    ee2[q, :NV] = x2
                    vec_copy(2, q).start()
                    scaled = (pos[q:q + 1, :] * x2.astype(F32)).astype(BF16)
                    ee2[q, NV:] = scaled
                    x2_ref[:, q * W:(q + 1) * W] = x2
                else:
                    weight = pos[q:q + 1, :]
                    heat = weight * total[:NV] - total[NV:] + arriving
                    heat_ref[:, q * W:(q + 1) * W] = heat

        waiting = None
        for s in range(C // GROUP):
            sums = products(s)
            if LATE and waiting is not None:
                finish(s - 1, waiting)
            if not LATE:
                finish(s, sums)
            waiting = sums
        if LATE:
            finish(C // GROUP - 1, waiting)

        if app == 0:
            odd_pairs(NV, eo1)
        elif app == 1:
            for q in range(Q - 1):
                eo2[q] = straddle(ee2, q, 2 * NV)

    for app in range(3):
        for q in range(Q):
            vec_copy(app, q).wait_send()
            spill_copy(app, q).wait_send()


def hand_over(a_ref, b_ref, a_out, b_out, sem):
    copies = [pltpu.make_async_copy(a_ref, a_out, sem.at[0]),
              pltpu.make_async_copy(b_ref, b_out, sem.at[1])]
    for copy in copies:
        copy.start()
    for copy in copies:
        copy.wait()


def body(start_vectors, blocks, block_cols, positions):
    C, K, B = blocks.shape[0], blocks.shape[1], blocks.shape[2]
    NV = start_vectors.shape[0]
    Q, W = C // 2, 2 * B
    rows = -(-Q // 8) * 8
    vmem = pl.BlockSpec(memory_space=pltpu.VMEM)
    dma = pltpu.SemaphoreType.DMA
    pairs = lambda count, m: pltpu.VMEM((count, m, W), BF16)
    results = pl.pallas_call(
        kernel,
        out_shape=(jax.ShapeDtypeStruct(start_vectors.shape, BF16),
                   jax.ShapeDtypeStruct(start_vectors.shape, F32)),
        in_specs=[vmem, vmem, vmem, pl.BlockSpec(memory_space=pl.ANY)],
        out_specs=(vmem, vmem),
        scratch_shapes=[
            pltpu.VMEM((C, K + 1, B, B), BF16), pltpu.VMEM((C, K + 1, B, B), BF16),
            pairs(3 * Q, NV), pairs(3 * Q, NV),
            pairs(2 * Q, NV), pairs(2 * Q, NV),
            pairs(2 * Q, NV), pairs(2 * Q, NV),
            pairs(2 * Q, 2 * NV), pairs(2 * Q, 2 * NV),
            pltpu.VMEM((C, 2 * NV, B), F32),
            pltpu.VMEM((3, Q, NV, W), BF16), pltpu.VMEM((3, Q, NV, W), BF16),
            pltpu.VMEM((rows, W), F32), pltpu.VMEM((rows, W), F32),
            pltpu.VMEM((C, 128), jnp.int32), pltpu.SMEM((C, 128), jnp.int32),
            dma((C,)), dma((3, Q)), dma((3, Q)), dma((3, Q)), dma((3, Q)),
            dma, dma, dma,
        ],
        compiler_params=pltpu.CompilerParams(
            collective_id=0, has_side_effects=True, vmem_limit_bytes=56 * 1024 * 1024),
    )(block_cols, start_vectors, positions.reshape(-1, 128), blocks)
    anywhere = pl.BlockSpec(memory_space=pl.ANY)
    return tuple(pl.pallas_call(
        hand_over,
        out_shape=tuple(jax.ShapeDtypeStruct(r.shape, r.dtype) for r in results),
        in_specs=[vmem, vmem],
        out_specs=(anywhere, anywhere),
        scratch_shapes=[dma((2,))],
    )(*results))


def solution(mesh):
    return jax.shard_map(
        body,
        mesh=mesh,
        in_specs=(
            P(None, ("grp", "row")),
            P(("grp", "row"), None, None, None),
            P(("grp", "row"), None),
            P(("grp", "row")),
        ),
        out_specs=(P(None, ("grp", "row")), P(None, ("grp", "row"))),
        check_vma=False,
    )
```

```python
import jax
import jax.numpy as jnp
from jax import lax
from jax.experimental import pallas as pl
from jax.experimental.pallas import tpu as pltpu
from jax.sharding import PartitionSpec as P

F32 = jnp.float32
BF16 = jnp.bfloat16
STEP = 6
GROUP = 2
LATE = True


def kernel(cols_ref, v_ref, p_ref, blocks_ref, x2_ref, heat_ref,
           blk, blkt, ze, zo, ee0, eo0, ee1, eo1, ee2, eo2, own, sout, sin,
           pos, pup, tabv, table,
           blk_sem, vs_sem, vr_sem, ss_sem, sr_sem, ps_sem, pr_sem, tab_sem):
    C, K = blocks_ref.shape[0], blocks_ref.shape[1]
    B = blocks_ref.shape[2]
    NV = v_ref.shape[0]
    Q = C // 2
    W = 2 * B
    n = lax.axis_size("row")
    me = lax.axis_index("row")
    nxt, prv = lax.rem(me + 1, n), lax.rem(me + n - 1, n)

    barrier = pltpu.get_barrier_semaphore()
    for neighbour in (prv, nxt):
        pl.semaphore_signal(barrier, inc=1, device_id={"row": neighbour},
                            device_id_type=pl.DeviceIdType.MESH)

    def block_copy(i):
        return pltpu.make_async_copy(
            blocks_ref.at[i], blk.at[i, pl.ds(0, K)], blk_sem.at[i])

    for i in range(C):
        block_copy(i).start()

    clusters = C * n
    off = cols_ref[...] - (me * C + lax.broadcasted_iota(jnp.int32, (C, K), 0))
    off = jnp.where(off < 0, off + clusters, off)
    lane = lax.broadcasted_iota(jnp.int32, (C, 128), 1)
    found = jnp.full((C, 128), K, jnp.int32)
    for k in range(K):
        found = jnp.where(off[:, k:k + 1] == lane, k, found)
    tabv[...] = found
    table_copy = pltpu.make_async_copy(tabv, table, tab_sem)
    table_copy.start()

    for q in range(Q):
        pair = v_ref[:, q * W:(q + 1) * W]
        ee0[q] = pair
        ze[Q + q, :NV] = pair
    pos[...] = jnp.zeros(pos.shape, F32)
    lines = p_ref[...].astype(F32)
    for q in range(Q):
        pos[q:q + 1, :] = jnp.concatenate(
            [lines[r:r + 1] for r in range(q * W // 128, (q + 1) * W // 128)], axis=1)

    def vec_copy(app, q):
        e = (ee0, ee1, ee2)[app]
        return pltpu.make_async_remote_copy(
            src_ref=e.at[q, pl.ds(0, NV)], dst_ref=e.at[Q + q, pl.ds(0, NV)],
            send_sem=vs_sem.at[app, q], recv_sem=vr_sem.at[app, q],
            device_id={"row": prv}, device_id_type=pl.DeviceIdType.MESH)

    def spill_copy(app, q):
        return pltpu.make_async_remote_copy(
            src_ref=sout.at[app, q], dst_ref=sin.at[app, q],
            send_sem=ss_sem.at[app, q], recv_sem=sr_sem.at[app, q],
            device_id={"row": nxt}, device_id_type=pl.DeviceIdType.MESH)

    pl.semaphore_wait(barrier, 2)
    for q in range(Q):
        vec_copy(0, q).start()
    pos_copy = pltpu.make_async_remote_copy(
        src_ref=pos, dst_ref=pup, send_sem=ps_sem, recv_sem=pr_sem,
        device_id={"row": prv}, device_id_type=pl.DeviceIdType.MESH)
    pos_copy.start()

    def straddle(ref, q, rows):
        return jnp.concatenate([ref[q, :rows, B:], ref[q + 1, :rows, :B]], axis=1)

    for q in range(Q):
        ze[q] = jnp.zeros(ze.shape[1:], BF16)
        ze[2 * Q + q] = jnp.zeros(ze.shape[1:], BF16)
        if q < Q - 1:
            zo[q] = jnp.zeros(zo.shape[1:], BF16)
            zo[2 * Q + q] = jnp.zeros(zo.shape[1:], BF16)

    def odd_pairs(rows, eo):
        for q in range(Q - 1, 2 * Q):
            odd = straddle(ze, q, rows)
            zo[q, :rows] = odd
            if Q <= q < 2 * Q - 1:
                eo[q - Q] = odd

    odd_pairs(NV, eo0)

    for i in range(C):
        blk[i, K] = jnp.zeros((B, B), BF16)
        blkt[i, K] = jnp.zeros((B, B), BF16)

    @pl.loop(0, C)
    def _(i):
        block_copy(i).wait()
        for k in range(K):
            blkt[i, k] = blk[i, k].T

    table_copy.wait()

    def across(ref, start, rows):
        return [ref[start + m, :rows] for m in range(Q)]

    for app, (ee, eo) in enumerate(((ee0, eo0), (ee1, eo1), (ee2, eo2))):
        M = 2 * NV if app == 2 else NV
        if app == 2:
            pos_copy.wait()

        if app < 2:
            @pl.loop(0, C // STEP)
            def _(s):
                spills = []
                for h in range(STEP):
                    j = STEP * s + h
                    t = (STEP // 2) * s + h // 2
                    z = (ze, zo)[h % 2]
                    lhs = jnp.concatenate(
                        [jnp.concatenate(across(z, t, M), axis=1),
                         jnp.concatenate(across(z, t + Q, M), axis=1)], axis=0)
                    rows = [lax.rem(j + C - d, C) for d in range(K, 0, -1)]
                    rhs = jnp.concatenate(
                        [blk[i, table[i, K - m]] for m, i in enumerate(rows)], axis=0)
                    acc = jnp.dot(lhs, rhs, preferred_element_type=F32)
                    own[j, :M] = acc[:M]
                    spills.append(acc[M:])
                    if h % 2:
                        sout[app, t] = jnp.concatenate(spills[-2:], axis=1).astype(BF16)
                        spill_copy(app, t).start()

        else:
            def mirrored(j, low, high):
                count = high - low
                src = eo if low % 2 else ee
                parts = [src[low // 2 + m] for m in range(count // 2)]
                if count % 2:
                    last = ee[(high - 1) // 2]
                    parts.append(last[:, :B] if high % 2 else last[:, B:])
                lhs = jnp.concatenate(parts, axis=1)
                rhs = jnp.concatenate(
                    [blk[i, table[i, (j - i) % C if j != i else C]]
                     for i in range(low, high)], axis=0)
                return jnp.dot(lhs, rhs, preferred_element_type=F32)

            for q in range(Q):
                pair = []
                for j in (2 * q, 2 * q + 1):
                    pair.append(mirrored(j, j, C))
                    if j:
                        own[j] = mirrored(j, 0, j)
                    else:
                        own[j] = jnp.zeros(own.shape[1:], F32)
                spill = jnp.concatenate(pair, axis=1)
                spill = pup[q:q + 1, :] * spill[:NV] - spill[NV:]
                sout[app, q] = spill.astype(BF16)
                spill_copy(app, q).start()

        def products(s):
            for g in range(GROUP // 2):
                q = (GROUP // 2) * s + g
                vec_copy(app, q).wait_recv()
                if app == 2:
                    up = pup[q:q + 1, :] * ee[Q + q, :NV].astype(F32)
                    ee[Q + q, NV:] = up.astype(BF16)
                eo[Q - 1 + q] = straddle(ee, Q - 1 + q, M)
            sums = []
            for h in range(GROUP):
                j = GROUP * s + h
                t = (GROUP // 2) * s + h // 2
                last = ee[t + Q]
                last = last[:, B:] if h % 2 else last[:, :B]
                lhs = jnp.concatenate(
                    across((ee, eo)[h % 2], t, M) + [last], axis=1)
                rhs = jnp.concatenate(
                    [blkt[j, table[j, d]] for d in range(K + 1)], axis=0)
                sums.append(own[j, :M] + jnp.dot(
                    lhs, rhs, preferred_element_type=F32))
            return sums

        def finish(s, sums):
            for g in range(GROUP // 2):
                q = (GROUP // 2) * s + g
                total = jnp.concatenate(sums[2 * g:2 * g + 2], axis=1)
                spill_copy(app, q).wait_recv()
                arriving = sin[app, q].astype(F32)
                if app == 0:
                    x1 = (total + arriving).astype(BF16)
                    ee1[q] = x1
                    vec_copy(1, q).start()
                    ze[Q + q, :NV] = x1
                elif app == 1:
                    x2 = 2.0 * (total + arriving) - ee0[q].astype(F32)
                    x2 = x2.astype(BF16)
                    ee2[q, :NV] = x2
                    vec_copy(2, q).start()
                    scaled = (pos[q:q + 1, :] * x2.astype(F32)).astype(BF16)
                    ee2[q, NV:] = scaled
                    x2_ref[:, q * W:(q + 1) * W] = x2
                else:
                    weight = pos[q:q + 1, :]
                    heat = weight * total[:NV] - total[NV:] + arriving
                    heat_ref[:, q * W:(q + 1) * W] = heat

        waiting = None
        for s in range(C // GROUP):
            sums = products(s)
            if LATE and waiting is not None:
                finish(s - 1, waiting)
            if not LATE:
                finish(s, sums)
            waiting = sums
        if LATE:
            finish(C // GROUP - 1, waiting)

        if app == 0:
            odd_pairs(NV, eo1)
        elif app == 1:
            for q in range(Q - 1):
                eo2[q] = straddle(ee2, q, 2 * NV)

    for app in range(3):
        for q in range(Q):
            vec_copy(app, q).wait_send()
            spill_copy(app, q).wait_send()


def hand_over(a_ref, b_ref, a_out, b_out, sem):
    copies = [pltpu.make_async_copy(a_ref, a_out, sem.at[0]),
              pltpu.make_async_copy(b_ref, b_out, sem.at[1])]
    for copy in copies:
        copy.start()
    for copy in copies:
        copy.wait()


def body(start_vectors, blocks, block_cols, positions):
    C, K, B = blocks.shape[0], blocks.shape[1], blocks.shape[2]
    NV = start_vectors.shape[0]
    Q, W = C // 2, 2 * B
    rows = -(-Q // 8) * 8
    vmem = pl.BlockSpec(memory_space=pltpu.VMEM)
    dma = pltpu.SemaphoreType.DMA
    pairs = lambda count, m: pltpu.VMEM((count, m, W), BF16)
    results = pl.pallas_call(
        kernel,
        out_shape=(jax.ShapeDtypeStruct(start_vectors.shape, BF16),
                   jax.ShapeDtypeStruct(start_vectors.shape, F32)),
        in_specs=[vmem, vmem, vmem, pl.BlockSpec(memory_space=pl.ANY)],
        out_specs=(vmem, vmem),
        scratch_shapes=[
            pltpu.VMEM((C, K + 1, B, B), BF16), pltpu.VMEM((C, K + 1, B, B), BF16),
            pairs(3 * Q, NV), pairs(3 * Q, NV),
            pairs(2 * Q, NV), pairs(2 * Q, NV),
            pairs(2 * Q, NV), pairs(2 * Q, NV),
            pairs(2 * Q, 2 * NV), pairs(2 * Q, 2 * NV),
            pltpu.VMEM((C, 2 * NV, B), F32),
            pltpu.VMEM((3, Q, NV, W), BF16), pltpu.VMEM((3, Q, NV, W), BF16),
            pltpu.VMEM((rows, W), F32), pltpu.VMEM((rows, W), F32),
            pltpu.VMEM((C, 128), jnp.int32), pltpu.SMEM((C, 128), jnp.int32),
            dma((C,)), dma((3, Q)), dma((3, Q)), dma((3, Q)), dma((3, Q)),
            dma, dma, dma,
        ],
        compiler_params=pltpu.CompilerParams(
            collective_id=0, has_side_effects=True, vmem_limit_bytes=56 * 1024 * 1024),
    )(block_cols, start_vectors, positions.reshape(-1, 128), blocks)
    anywhere = pl.BlockSpec(memory_space=pl.ANY)
    return tuple(pl.pallas_call(
        hand_over,
        out_shape=tuple(jax.ShapeDtypeStruct(r.shape, r.dtype) for r in results),
        in_specs=[vmem, vmem],
        out_specs=(anywhere, anywhere),
        scratch_shapes=[dma((2,))],
    )(*results))


def solution(mesh):
    return jax.shard_map(
        body,
        mesh=mesh,
        in_specs=(
            P(None, ("grp", "row")),
            P(("grp", "row"), None, None, None),
            P(("grp", "row"), None),
            P(("grp", "row")),
        ),
        out_specs=(P(None, ("grp", "row")), P(None, ("grp", "row"))),
        check_vma=False,
    )
```
